128 devices in a mesh: dev: 128 (over z, x, y, core).
Axes of the slice: x: 4, y: 4, z: 4, core: 2. Of those that a mesh axis runs over, the one named last changes fastest.
Arguments:
- features: float32 [65536, 256], P('dev'), may hold values from -6 to 6
- keep: int32 [65536], P('dev'), may hold values 0 or 1
- theta_one: float32 [256, 256], replicated, may hold values from -0.375 to 0.375
- theta_two: float32 [256, 256], replicated, may hold values from -0.375 to 0.375
- cotangent: float32 [65536, 256], P('dev'), may hold values from -6 to 6
- send_node: int32 [128, 128, 4], P('dev'), may hold values from 0 to 511
- recv_edge: int32 [128, 128, 4], P('dev'), may hold values from 0 to 255
- send_count: int32 [128, 128], P('dev'), may hold values from 0 to 4, as said below
Outputs:
- grad_features: float32 [65536, 256], P('dev')
- grad_theta_one: float32 [256, 256], replicated
- grad_theta_two: float32 [256, 256], replicated
The draws below stay inside these ranges and needn't reach their ends.
Inputs may be any that keep to these rules, and one draw needn't show every extreme that they name: `send_count`: each source device has 4 live slots to at least one destination.
All inputs are finite; a program needn't handle non-finite values. No bound on the sum of `keep` on one device may be relied on, other than what follows from the above.
Results may differ from the reference program's by a relative error of at most 0.0003.
Values sent between devices are 32-bit elements; how exact they have to be, the bound alone decides.
A program may use at most 64 MiB of HBM per device.

```python
import jax
import jax.numpy as jnp
from jax import lax

C = 256
NODES_DEV = 512
EDGES_DEV = 256
PEERS = 128
CAP = 4
NODES = 65536
EDGES = 32768


def draw_send_count(key, part):
    key = jax.random.fold_in(key, 5)
    key_hot, key_low, key_high, key_pick = jax.random.split(key, 4)
    hot_rows = jax.random.randint(key_hot, (PEERS,), 0, 3) == 0
    lower = jax.random.randint(key_low, (PEERS, PEERS), 0, CAP // 2 + 1)
    higher = jax.random.randint(key_high, (PEERS, PEERS), CAP // 2, CAP + 1)
    counts = jnp.where(hot_rows[None, :], higher, lower)
    picked = jax.random.randint(key_pick, (PEERS,), 0, PEERS)
    columns = jnp.arange(PEERS)[None, :]
    counts = jnp.where(columns == picked[:, None], CAP, counts)
    return counts.astype(jnp.int32)


def plant(entries, rng, least, high):
    dims = entries.shape
    place = [jax.random.randint(jax.random.fold_in(rng, axis), (), 0, dims[axis]) for axis in range(len(dims))]
    entries = entries.at[tuple(place)].set(least)
    longest = dims.index(max(dims))
    place[longest] = (place[longest] + 1) % dims[longest]
    return entries.at[tuple(place)].set(high)


def block_levels(rng, shape, cuts, smallest, top_value):
    loudness = 1.0
    for position, shards_of in cuts:
        steps = jax.random.uniform(jax.random.fold_in(jax.random.fold_in(rng, 6), position), (shards_of,), jnp.float32, smallest / len(cuts), top_value / len(cuts))
        loudness = loudness * jnp.repeat(jnp.exp(steps), shape[position] // shards_of).reshape((-1,) + (1,) * (len(shape) - 1 - position))
    return loudness


def noise(rng, shape, deviation, bound, shards=(), kind=jnp.bfloat16):
    values = deviation * jax.random.normal(rng, shape, jnp.float32)
    if shards:
        values = values * block_levels(rng, shape, shards, -0.22, 0.18)
    return jnp.clip(values, -bound, bound).astype(kind)


def setup_inputs(seed: int = 0) -> dict:
    key_of = jax.random.split(jax.random.key(seed), 9)
    features = noise(key_of[0], (NODES, C), 1.0, 6.0, ((0, 128),), jnp.float32)
    keep = plant((jax.random.randint(key_of[1], (NODES,), 0, 5) < 4).astype(jnp.int32), jax.random.fold_in(key_of[1], 1), 0, 1)
    theta_one = noise(key_of[2], (C, C), C ** -0.5, 0.375, (), jnp.float32)
    theta_two = noise(key_of[3], (C, C), C ** -0.5, 0.375, (), jnp.float32)
    cotangent = noise(key_of[4], (NODES, C), 1.0, 6.0, ((0, 128),), jnp.float32)
    send_node = plant(jax.random.randint(key_of[5], (PEERS, PEERS, CAP), 0, NODES_DEV), jax.random.fold_in(key_of[5], 1), 0, NODES_DEV - 1).astype(jnp.int32)
    recv_edge = plant(jax.random.randint(key_of[6], (PEERS, PEERS, CAP), 0, EDGES_DEV), jax.random.fold_in(key_of[6], 1), 0, EDGES_DEV - 1).astype(jnp.int32)
    send_count = draw_send_count(jax.random.fold_in(key_of[8], 71), 0)
    return dict(features=features, keep=keep, theta_one=theta_one, theta_two=theta_two, cotangent=cotangent, send_node=send_node, recv_edge=recv_edge, send_count=send_count)


def matmul(left, right):
    return jnp.dot(left, right, preferred_element_type=jnp.float32, precision=lax.Precision.HIGHEST)

def propagate(field, node_ids, edge_ids, live, node_scale, edge_scale):
    scaled = field * node_scale[:, None]
    messages = scaled[node_ids] * live[:, None]
    edge_sums = jax.ops.segment_sum(messages, edge_ids, num_segments=EDGES) * edge_scale[:, None]
    returned = edge_sums[edge_ids] * live[:, None]
    return jax.ops.segment_sum(returned, node_ids, num_segments=NODES) * node_scale[:, None]

def reference(features, keep, theta_one, theta_two, cotangent, send_node, recv_edge, send_count):
    source = lax.broadcasted_iota(jnp.int32, (PEERS, PEERS, CAP), 0)
    target = lax.broadcasted_iota(jnp.int32, (PEERS, PEERS, CAP), 1)
    slot_pos = lax.broadcasted_iota(jnp.int32, (PEERS, PEERS, CAP), 2)
    node_ids = (source * NODES_DEV + send_node).reshape(-1).astype(jnp.int32)
    edge_ids = (target * EDGES_DEV + jnp.transpose(recv_edge, (1, 0, 2))).reshape(-1).astype(jnp.int32)
    live = (slot_pos < send_count[:, :, None]).astype(jnp.float32).reshape(-1)
    node_degree = jax.ops.segment_sum(live, node_ids, num_segments=NODES)
    edge_degree = jax.ops.segment_sum(live, edge_ids, num_segments=EDGES)
    node_scale = 1.0 / jnp.sqrt(jnp.maximum(node_degree, 1.0))
    edge_scale = 1.0 / jnp.maximum(edge_degree, 1.0)
    keep_f = keep.astype(jnp.float32)[:, None]
    dropped = features * keep_f
    spread_in = propagate(dropped, node_ids, edge_ids, live, node_scale, edge_scale)
    pre = matmul(spread_in, theta_one)
    hidden = jax.nn.elu(pre)
    spread_hidden = propagate(hidden, node_ids, edge_ids, live, node_scale, edge_scale)
    spread_cot = propagate(cotangent, node_ids, edge_ids, live, node_scale, edge_scale)
    norm_factor = 1.0 / jnp.sqrt(jnp.float32(NODES))
    grad_theta_two = matmul(spread_hidden.T, cotangent) * norm_factor
    slope = jnp.where(pre > 0, 1.0, jnp.exp(jnp.minimum(pre, 0.0)))
    grad_pre = matmul(spread_cot, theta_two.T) * slope
    grad_theta_one = matmul(spread_in.T, grad_pre) * norm_factor
    spread_grad = propagate(grad_pre, node_ids, edge_ids, live, node_scale, edge_scale)
    grad_features = matmul(spread_grad, theta_one.T) * keep_f
    return (grad_features, grad_theta_one, grad_theta_two)
```

```python
import functools

import jax
import jax.numpy as jnp
from jax import lax
from jax.experimental import pallas as pl
from jax.experimental.pallas import tpu as pltpu
from jax.sharding import PartitionSpec as P

MESH = pl.DeviceIdType.MESH
F32, BF16 = jnp.float32, jnp.bfloat16
UNROLL = 8
A_DOWN, B_DOWN, A_UP, B_UP, C_DOWN, C_UP, PAIR_IN, SCATTER, GATHER, PAIR_OUT = range(10)


def split(x):
    high = x.astype(BF16)
    return high, (x - high.astype(F32)).astype(BF16)


def dot(left, right, dims=((1,), (0,))):
    return lax.dot_general(left, right, (dims, ((), ())), preferred_element_type=F32)


def pick(onehot, x):
    high, low = split(x)
    return dot(onehot, high) + dot(onehot, low)


def matmul(left, right, dims=((1,), (0,))):
    lh, ll = split(left)
    rh, rl = split(right)
    return dot(lh, rh, dims) + (dot(lh, rl, dims) + dot(ll, rh, dims))


def kernel(
    n, slots, features, keep, theta_one, theta_two, cotangent, send_node, recv_edge, send_count,
    grad_features, grad_one, grad_two,
    gather, spread, meet, out, back, terms, partner, pair_sum, parts, total, send_sem, recv_sem,
):
    me = lax.axis_index("dev")
    core, chip, chips = lax.rem(me, 2), me // 2, n // 2
    other = me + 1 - 2 * core
    nodes, width = features.shape
    lanes = width // 2
    tile = 2 * slots

    barrier = pltpu.get_barrier_semaphore()

    def greet(_, peer):
        peer = lax.rem(peer + 1, n)
        pl.semaphore_signal(barrier, inc=1, device_id=(peer,), device_id_type=MESH)
        return peer

    lax.fori_loop(0, n - 1, greet, me, unroll=UNROLL)

    def block(index, rows=tile):
        return pl.ds(pl.multiple_of(index * rows, rows), rows)

    def exchange(phase, src, dst):
        def push(_, peer):
            peer = lax.rem(peer + 1, n)
            pltpu.make_async_remote_copy(
                src_ref=src.at[block(peer)],
                dst_ref=dst.at[block(me)],
                send_sem=send_sem.at[phase],
                recv_sem=recv_sem.at[phase],
                device_id=(peer,),
                device_id_type=MESH,
            ).start()
            return peer

        lax.fori_loop(0, n - 1, push, me, unroll=UNROLL)
        pltpu.make_async_copy(src.at[block(me)], dst.at[block(me)], recv_sem.at[phase]).start()

    def chip_exchange(phase, src_block, dst):
        def push(_, peer):
            peer = lax.rem(peer + 2, n)
            pltpu.make_async_remote_copy(
                src_ref=src_block(peer // 2),
                dst_ref=dst.at[block(chip)],
                send_sem=send_sem.at[phase],
                recv_sem=recv_sem.at[phase],
                device_id=(peer,),
                device_id_type=MESH,
            ).start()
            return peer

        lax.fori_loop(0, chips - 1, push, me, unroll=UNROLL)
        pltpu.make_async_copy(src_block(chip), dst.at[block(chip)], recv_sem.at[phase]).start()

    def arrived(phase, ref):
        pltpu.make_async_copy(ref, ref, recv_sem.at[phase]).wait()

    def sent(phase, ref):
        pltpu.make_async_copy(ref, ref, send_sem.at[phase]).wait()

    def put(ref, j, rows):
        for h in range(2):
            ref[pl.ds(h * slots + j, n, stride=tile), :] = rows[:, h * lanes : (h + 1) * lanes]

    def get(ref, j):
        return [ref[pl.ds(h * slots + j, n, stride=tile), :] for h in range(2)]

    def take(ref):
        return jnp.concatenate([jnp.concatenate(get(ref, j), axis=1) for j in range(slots)], axis=0)

    eye = lax.broadcasted_iota(jnp.int32, (n, n), 0) == lax.broadcasted_iota(jnp.int32, (n, n), 1)

    def as_row(column):
        return jnp.sum(jnp.where(eye, column, 0.0), axis=0, keepdims=True)

    def as_column(row):
        return jnp.sum(jnp.where(eye, row, 0.0), axis=1, keepdims=True)

    count = send_count[...].astype(F32)
    node_of = send_node[0].astype(F32)
    edge_of = recv_edge[0].astype(F32)
    node_lane = lax.broadcasted_iota(jnp.int32, (n, nodes), 1).astype(F32)
    node_row = lax.broadcasted_iota(jnp.int32, (nodes, n), 0).astype(F32)
    degree = jnp.zeros((nodes, n), F32)
    live = []
    for j in range(slots):
        mine = jnp.where(count > j, node_of[j : j + 1], -1.0)
        mine_column = as_column(mine)
        live.append(mine_column >= 0.0)
        gather[j * n : (j + 1) * n, :] = (node_lane == mine_column).astype(F32).astype(BF16)
        here = (node_row == mine).astype(F32)
        degree += here
        spread[:, j * n : (j + 1) * n] = here.astype(BF16)
    edge_cols = [as_column(edge_of[j : j + 1]) for j in range(slots)]
    edge_row = jnp.concatenate([edge_of[j : j + 1] for j in range(slots)], axis=1)
    for j in range(slots):
        meet[j * n : (j + 1) * n, :] = (edge_row == edge_cols[j]).astype(F32).astype(BF16)
    degree = jnp.sum(degree, axis=1, keepdims=True)
    node_scale = 1.0 / jnp.sqrt(jnp.maximum(degree, 1.0))
    keep_rows = keep[...].astype(F32)
    keep_f = jnp.concatenate([as_column(keep_rows[r : r + 1]) for r in range(nodes // n)], axis=0)

    def load_out(ref, field, mark):
        rows = pick(gather[...], field * node_scale)
        for j in range(slots):
            part = rows[j * n : (j + 1) * n]
            put(ref, j, jnp.where(live[j], part, jnp.inf) if mark else part)

    load_out(out.at[A_DOWN], features[...] * keep_f, True)
    pl.semaphore_wait(barrier, n - 1)
    exchange(A_DOWN, out.at[A_DOWN], back.at[A_DOWN])
    load_out(out.at[B_DOWN], cotangent[...], False)
    exchange(B_DOWN, out.at[B_DOWN], back.at[B_DOWN])

    arrived(A_DOWN, back.at[A_DOWN])
    fields, alive = [], []
    for j in range(slots):
        halves = get(back.at[A_DOWN], j)
        is_live = halves[0][:, :1] < jnp.inf
        alive.append(is_live.astype(F32))
        fields.append(jnp.where(is_live, jnp.concatenate(halves, axis=1), 0.0))
    alive_row = jnp.concatenate([as_row(a) for a in alive], axis=1)
    edge_scale = []
    for j in range(slots):
        shared = jnp.where(edge_row == edge_cols[j], alive_row, 0.0)
        edge_scale.append(1.0 / jnp.maximum(jnp.sum(shared, axis=1, keepdims=True), 1.0))

    def load_back(ref, field):
        rows = pick(meet[...], field)
        for j in range(slots):
            put(ref, j, rows[j * n : (j + 1) * n] * edge_scale[j])

    load_back(out.at[A_UP], jnp.concatenate(fields, axis=0))
    exchange(A_UP, out.at[A_UP], back.at[A_UP])
    arrived(B_DOWN, back.at[B_DOWN])
    load_back(out.at[B_UP], take(back.at[B_DOWN]))
    exchange(B_UP, out.at[B_UP], back.at[B_UP])

    arrived(A_UP, back.at[A_UP])
    spread_in = pick(spread[...], take(back.at[A_UP])) * node_scale
    pre = matmul(spread_in, theta_one[...])
    grow = jnp.exp(jnp.minimum(pre, 0.0))
    hidden = jnp.where(pre > 0, pre, grow - 1.0)
    slope = jnp.where(pre > 0, 1.0, grow)
    arrived(B_UP, back.at[B_UP])
    spread_cot = pick(spread[...], take(back.at[B_UP])) * node_scale
    grad_pre = matmul(spread_cot, theta_two[...], ((1,), (1,))) * slope
    load_out(out.at[C_DOWN], grad_pre, False)
    exchange(C_DOWN, out.at[C_DOWN], back.at[C_DOWN])

    term_one = matmul(spread_in, grad_pre, ((0,), (0,)))
    term_two = matmul(hidden, spread_cot, ((0,), (0,)))
    for k, term in enumerate((term_one, term_two)):
        for h in range(2):
            terms[k, h * width : (h + 1) * width, :] = term[:, h * lanes : (h + 1) * lanes]
    pltpu.make_async_remote_copy(
        src_ref=terms.at[1 - core],
        dst_ref=partner,
        send_sem=send_sem.at[PAIR_IN],
        recv_sem=recv_sem.at[PAIR_IN],
        device_id=(other,),
        device_id_type=MESH,
    ).start()
    arrived(PAIR_IN, partner)
    pair_sum[...] = terms[core] + partner[...]
    chip_exchange(SCATTER, lambda q: pair_sum.at[block(q)], parts)

    arrived(C_DOWN, back.at[C_DOWN])
    load_back(out.at[C_UP], take(back.at[C_DOWN]))
    exchange(C_UP, out.at[C_UP], back.at[C_UP])

    arrived(SCATTER, parts)
    sent(SCATTER, parts.at[pl.ds(0, (chips - 1) * tile)])
    norm_factor = 1.0 / jnp.sqrt(jnp.float32(nodes * n))
    summed = jnp.sum(parts[...].reshape(chips, tile, lanes), axis=0) * norm_factor
    pair_sum[:tile, :] = summed
    chip_exchange(GATHER, lambda q: pair_sum.at[pl.ds(0, tile)], total.at[core])

    arrived(C_UP, back.at[C_UP])
    spread_grad = pick(spread[...], take(back.at[C_UP])) * node_scale
    grad_features[...] = matmul(spread_grad, theta_one[...], ((1,), (1,))) * keep_f

    arrived(GATHER, total.at[core])
    pltpu.make_async_remote_copy(
        src_ref=total.at[core],
        dst_ref=total.at[core],
        send_sem=send_sem.at[PAIR_OUT],
        recv_sem=recv_sem.at[PAIR_OUT],
        device_id=(other,),
        device_id_type=MESH,
    ).start()
    for phase in (A_DOWN, B_DOWN, A_UP, B_UP, C_DOWN, C_UP):
        sent(phase, out.at[phase, pl.ds(0, (n - 1) * tile)])
    sent(PAIR_IN, partner)
    sent(GATHER, parts.at[pl.ds(0, (chips - 1) * tile)])
    sent(PAIR_OUT, partner)
    arrived(PAIR_OUT, partner)
    for k, ref in enumerate((grad_one, grad_two)):
        for h in range(2):
            ref[:, h * lanes : (h + 1) * lanes] = total[k, h * width : (h + 1) * width, :]


def solution(mesh):
    n = mesh.shape["dev"]

    def body(features, keep, theta_one, theta_two, cotangent, send_node, recv_edge, send_count):
        nodes, width = features.shape
        slots = send_node.shape[2]
        rows = n * 2 * slots
        whole = pl.BlockSpec(memory_space=pltpu.VMEM)
        return pl.pallas_call(
            functools.partial(kernel, n, slots),
            out_shape=(
                jax.ShapeDtypeStruct((nodes, width), F32),
                jax.ShapeDtypeStruct((width, width), F32),
                jax.ShapeDtypeStruct((width, width), F32),
            ),
            in_specs=[whole] * 8,
            out_specs=(whole,) * 3,
            scratch_shapes=[
                pltpu.VMEM((slots * n, nodes), BF16),
                pltpu.VMEM((nodes, slots * n), BF16),
                pltpu.VMEM((slots * n, slots * n), BF16),
                pltpu.VMEM((6, rows, width // 2), F32),
                pltpu.VMEM((6, rows, width // 2), F32),
                pltpu.VMEM((2, 2 * width, width // 2), F32),
                pltpu.VMEM((2 * width, width // 2), F32),
                pltpu.VMEM((2 * width, width // 2), F32),
                pltpu.VMEM((2 * width, width // 2), F32),
                pltpu.VMEM((2, 2 * width, width // 2), F32),
                pltpu.SemaphoreType.DMA((10,)),
                pltpu.SemaphoreType.DMA((10,)),
            ],
            compiler_params=pltpu.CompilerParams(
                collective_id=0, has_side_effects=True, vmem_limit_bytes=48 << 20
            ),
        )(
            features, keep.reshape(nodes // n, n), theta_one, theta_two, cotangent,
            send_node.transpose(0, 2, 1), recv_edge.transpose(0, 2, 1), send_count,
        )

    placed = (
        P("dev", None),
        P("dev"),
        P(),
        P(),
        P("dev", None),
        P("dev", None, None),
        P("dev", None, None),
        P("dev", None),
    )
    return jax.shard_map(
        body, mesh=mesh, in_specs=placed, out_specs=(P("dev", None), P(), P()), check_vma=False
    )
```

```python
import functools

import jax
import jax.numpy as jnp
from jax import lax
from jax.experimental import pallas as pl
from jax.experimental.pallas import tpu as pltpu
from jax.sharding import PartitionSpec as P

MESH = pl.DeviceIdType.MESH
F32, BF16 = jnp.float32, jnp.bfloat16
ROW = 8
A_DOWN, B_DOWN, A_UP, B_UP, C_DOWN, C_UP, PAIR_IN, SCATTER, GATHER, PAIR_OUT = range(10)


SIDE = 4


def far_first():
    left = [(z, x, y) for z in range(SIDE) for x in range(SIDE) for y in range(SIDE)][1:]
    runs = []
    while left:
        z, x, y = left[0]
        run = []
        for step in ((z, x, y), (x, y, z), (y, z, x)):
            for there in (step, tuple(-v % SIDE for v in step)):
                if there not in run:
                    run.append(there)
        left = [there for there in left if there not in run]
        runs.append(run)
    return sorted(runs, key=lambda run: -sum(min(v, SIDE - v) for v in run[0]))


def split(x):
    high = x.astype(BF16)
    return high, (x - high.astype(F32)).astype(BF16)


def dot(left, right, dims=((1,), (0,))):
    return lax.dot_general(left, right, (dims, ((), ())), preferred_element_type=F32)


def pick(onehot, x):
    high, low = split(x)
    return dot(onehot, high) + dot(onehot, low)


def matmul(left, right, dims=((1,), (0,))):
    lh, ll = split(left)
    rh, rl = split(right)
    return dot(lh, rh, dims) + (dot(lh, rl, dims) + dot(ll, rh, dims))


def kernel(
    n, slots, *refs,
):
    given, (grad_features, grad_one, grad_two), held = refs[:8], refs[8:11], refs[11:19]
    (
        gather, spread, meet, out, back, terms, partner, pair_sum, parts, total, send_sem, recv_sem, load_sem,
        row_ready,
    ) = refs[19:]
    features, keep, theta_one, theta_two, cotangent, send_node, recv_edge, send_count = held
    loads = [pltpu.make_async_copy(given[i], held[i], load_sem.at[i]) for i in range(8)]
    for i in (5, 7, 6, 1, 0, 4, 2, 3):
        loads[i].start()
    me = lax.axis_index("dev")
    core, chip, chips = lax.rem(me, 2), me // 2, n // 2
    other = me + 1 - 2 * core
    place = (me // (2 * SIDE * SIDE), lax.rem(me // (2 * SIDE), SIDE), lax.rem(chip, SIDE))
    along = [
        [lax.rem(place[axis] + v, SIDE) * pitch for v in range(SIDE)]
        for axis, pitch in enumerate((2 * SIDE * SIDE, 2 * SIDE, 2))
    ]
    cores = (core, 1 - core)

    def peers(which):
        for run in far_first():
            for c in which:
                for z, x, y in run:
                    yield along[0][z] + along[1][x] + along[2][y] + c
    nodes, width = features.shape
    lanes = width // 2
    tile = 2 * slots

    barrier = pltpu.get_barrier_semaphore()
    row, column, rows, columns = me // ROW, lax.rem(me, ROW), n // ROW, ROW
    in_row = [row * columns + lax.rem(column + k, columns) for k in range(1, columns)]
    in_column = [lax.rem(row + k, rows) * columns + column for k in range(1, rows)]
    for peer in in_row + in_column:
        pl.semaphore_signal(barrier, inc=1, device_id=(peer,), device_id_type=MESH)

    def block(index, rows=tile):
        return pl.ds(pl.multiple_of(index * rows, rows), rows)

    def exchange(phase, src, dst):
        for peer in [*peers(cores), other]:
            pltpu.make_async_remote_copy(
                src_ref=src.at[block(peer)],
                dst_ref=dst.at[block(me)],
                send_sem=send_sem.at[phase],
                recv_sem=recv_sem.at[phase],
                device_id=(peer,),
                device_id_type=MESH,
            ).start()
        pltpu.make_async_copy(src.at[block(me)], dst.at[block(me)], recv_sem.at[phase]).start()

    def chip_exchange(phase, src_block, dst):
        for peer in peers((core,)):
            pltpu.make_async_remote_copy(
                src_ref=src_block(peer // 2),
                dst_ref=dst.at[block(chip)],
                send_sem=send_sem.at[phase],
                recv_sem=recv_sem.at[phase],
                device_id=(peer,),
                device_id_type=MESH,
            ).start()
        pltpu.make_async_copy(src_block(chip), dst.at[block(chip)], recv_sem.at[phase]).start()

    def arrived(phase, ref):
        pltpu.make_async_copy(ref, ref, recv_sem.at[phase]).wait()

    def sent(phase, ref):
        pltpu.make_async_copy(ref, ref, send_sem.at[phase]).wait()

    def put(ref, j, rows):
        for h in range(2):
            ref[pl.ds(h * slots + j, n, stride=tile), :] = rows[:, h * lanes : (h + 1) * lanes]

    def get(ref, j):
        return [ref[pl.ds(h * slots + j, n, stride=tile), :] for h in range(2)]

    def take(ref):
        return jnp.concatenate([jnp.concatenate(get(ref, j), axis=1) for j in range(slots)], axis=0)

    eye = lax.broadcasted_iota(jnp.int32, (n, n), 0) == lax.broadcasted_iota(jnp.int32, (n, n), 1)

    def as_row(column):
        return jnp.sum(jnp.where(eye, column, 0.0), axis=0, keepdims=True)

    def as_column(row):
        return jnp.sum(jnp.where(eye, row, 0.0), axis=1, keepdims=True)

    pl.semaphore_wait(barrier, rows + columns - 2)
    for peer in in_column:
        pl.semaphore_signal(row_ready, inc=1, device_id=(peer,), device_id_type=MESH)

    for i in (5, 7, 6, 1):
        loads[i].wait()
    count = send_count[...].astype(F32)
    node_of = send_node[0].astype(F32)
    edge_of = recv_edge[0].astype(F32)
    node_lane = lax.broadcasted_iota(jnp.int32, (n, nodes), 1).astype(F32)
    node_row = lax.broadcasted_iota(jnp.int32, (nodes, n), 0).astype(F32)
    degree = jnp.zeros((nodes, n), F32)
    live = []
    for j in range(slots):
        mine = jnp.where(count > j, node_of[j : j + 1], -1.0)
        mine_column = as_column(mine)
        live.append(mine_column >= 0.0)
        gather[j * n : (j + 1) * n, :] = (node_lane == mine_column).astype(F32).astype(BF16)
        here = (node_row == mine).astype(F32)
        degree += here
        spread[:, j * n : (j + 1) * n] = here.astype(BF16)
    edge_cols = [as_column(edge_of[j : j + 1]) for j in range(slots)]
    edge_row = jnp.concatenate([edge_of[j : j + 1] for j in range(slots)], axis=1)
    for j in range(slots):
        meet[j * n : (j + 1) * n, :] = (edge_row == edge_cols[j]).astype(F32).astype(BF16)
    degree = jnp.sum(degree, axis=1, keepdims=True)
    node_scale = 1.0 / jnp.sqrt(jnp.maximum(degree, 1.0))
    keep_rows = keep[...].astype(F32)
    keep_f = jnp.concatenate([as_column(keep_rows[r : r + 1]) for r in range(nodes // n)], axis=0)

    def load_out(ref, field, mark):
        rows = pick(gather[...], field * node_scale)
        for j in range(slots):
            part = rows[j * n : (j + 1) * n]
            put(ref, j, jnp.where(live[j], part, jnp.inf) if mark else part)

    loads[0].wait()
    load_out(out.at[A_DOWN], features[...] * keep_f, True)
    loads[4].wait()
    load_out(out.at[B_DOWN], cotangent[...], False)
    pl.semaphore_wait(row_ready, rows - 1)
    exchange(A_DOWN, out.at[A_DOWN], back.at[A_DOWN])
    exchange(B_DOWN, out.at[B_DOWN], back.at[B_DOWN])

    arrived(A_DOWN, back.at[A_DOWN])
    fields, alive = [], []
    for j in range(slots):
        halves = get(back.at[A_DOWN], j)
        is_live = halves[0][:, :1] < jnp.inf
        alive.append(is_live.astype(F32))
        fields.append(jnp.where(is_live, jnp.concatenate(halves, axis=1), 0.0))
    alive_row = jnp.concatenate([as_row(a) for a in alive], axis=1)
    edge_scale = []
    for j in range(slots):
        shared = jnp.where(edge_row == edge_cols[j], alive_row, 0.0)
        edge_scale.append(1.0 / jnp.maximum(jnp.sum(shared, axis=1, keepdims=True), 1.0))

    def load_back(ref, field):
        rows = pick(meet[...], field)
        for j in range(slots):
            put(ref, j, rows[j * n : (j + 1) * n] * edge_scale[j])

    load_back(out.at[A_UP], jnp.concatenate(fields, axis=0))
    exchange(A_UP, out.at[A_UP], back.at[A_UP])
    arrived(B_DOWN, back.at[B_DOWN])
    load_back(out.at[B_UP], take(back.at[B_DOWN]))
    exchange(B_UP, out.at[B_UP], back.at[B_UP])

    arrived(A_UP, back.at[A_UP])
    spread_in = pick(spread[...], take(back.at[A_UP])) * node_scale
    loads[2].wait()
    loads[3].wait()
    pre = matmul(spread_in, theta_one[...])
    grow = jnp.exp(jnp.minimum(pre, 0.0))
    hidden = jnp.where(pre > 0, pre, grow - 1.0)
    slope = jnp.where(pre > 0, 1.0, grow)
    arrived(B_UP, back.at[B_UP])
    spread_cot = pick(spread[...], take(back.at[B_UP])) * node_scale
    grad_pre = matmul(spread_cot, theta_two[...], ((1,), (1,))) * slope
    load_out(out.at[C_DOWN], grad_pre, False)
    exchange(C_DOWN, out.at[C_DOWN], back.at[C_DOWN])

    term_one = matmul(spread_in, grad_pre, ((0,), (0,)))
    term_two = matmul(hidden, spread_cot, ((0,), (0,)))
    for k, term in enumerate((term_one, term_two)):
        for h in range(2):
            terms[k, h * width : (h + 1) * width, :] = term[:, h * lanes : (h + 1) * lanes]
    pltpu.make_async_remote_copy(
        src_ref=terms.at[1 - core],
        dst_ref=partner,
        send_sem=send_sem.at[PAIR_IN],
        recv_sem=recv_sem.at[PAIR_IN],
        device_id=(other,),
        device_id_type=MESH,
    ).start()
    arrived(PAIR_IN, partner)
    pair_sum[...] = terms[core] + partner[...]
    chip_exchange(SCATTER, lambda q: pair_sum.at[block(q)], parts)

    arrived(C_DOWN, back.at[C_DOWN])
    load_back(out.at[C_UP], take(back.at[C_DOWN]))
    exchange(C_UP, out.at[C_UP], back.at[C_UP])

    arrived(SCATTER, parts)
    sent(SCATTER, parts.at[pl.ds(0, (chips - 1) * tile)])
    norm_factor = 1.0 / jnp.sqrt(jnp.float32(nodes * n))
    summed = jnp.sum(parts[...].reshape(chips, tile, lanes), axis=0) * norm_factor
    pair_sum[:tile, :] = summed
    chip_exchange(GATHER, lambda q: pair_sum.at[pl.ds(0, tile)], total.at[core])

    arrived(C_UP, back.at[C_UP])
    spread_grad = pick(spread[...], take(back.at[C_UP])) * node_scale
    grad_features[...] = matmul(spread_grad, theta_one[...], ((1,), (1,))) * keep_f

    arrived(GATHER, total.at[core])
    pltpu.make_async_remote_copy(
        src_ref=total.at[core],
        dst_ref=total.at[core],
        send_sem=send_sem.at[PAIR_OUT],
        recv_sem=recv_sem.at[PAIR_OUT],
        device_id=(other,),
        device_id_type=MESH,
    ).start()
    for phase in (A_DOWN, B_DOWN, A_UP, B_UP, C_DOWN, C_UP):
        sent(phase, out.at[phase, pl.ds(0, (n - 1) * tile)])
    sent(PAIR_IN, partner)
    sent(GATHER, parts.at[pl.ds(0, (chips - 1) * tile)])
    sent(PAIR_OUT, partner)
    arrived(PAIR_OUT, partner)
    for k, ref in enumerate((grad_one, grad_two)):
        for h in range(2):
            ref[:, h * lanes : (h + 1) * lanes] = total[k, h * width : (h + 1) * width, :]


def write_out(*refs):
    copies = [pltpu.make_async_copy(refs[i], refs[3 + i], refs[6].at[i]) for i in range(3)]
    for copy in copies:
        copy.start()
    for copy in copies:
        copy.wait()


def solution(mesh):
    n = mesh.shape["dev"]

    def body(features, keep, theta_one, theta_two, cotangent, send_node, recv_edge, send_count):
        nodes, width = features.shape
        slots = send_node.shape[2]
        rows = n * 2 * slots
        whole = pl.BlockSpec(memory_space=pltpu.VMEM)
        given = (
            features, keep.reshape(nodes // n, n), theta_one, theta_two, cotangent,
            send_node.transpose(0, 2, 1), recv_edge.transpose(0, 2, 1), send_count,
        )
        given = [pltpu.with_memory_space_constraint(x, pltpu.HBM) for x in given]
        results = pl.pallas_call(
            functools.partial(kernel, n, slots),
            out_shape=(
                jax.ShapeDtypeStruct((nodes, width), F32),
                jax.ShapeDtypeStruct((width, width), F32),
                jax.ShapeDtypeStruct((width, width), F32),
            ),
            in_specs=[pl.BlockSpec(memory_space=pltpu.HBM)] * 8,
            out_specs=(whole,) * 3,
            scratch_shapes=[pltpu.VMEM(x.shape, x.dtype) for x in given]
            + [
                pltpu.VMEM((slots * n, nodes), BF16),
                pltpu.VMEM((nodes, slots * n), BF16),
                pltpu.VMEM((slots * n, slots * n), BF16),
                pltpu.VMEM((6, rows, width // 2), F32),
                pltpu.VMEM((6, rows, width // 2), F32),
                pltpu.VMEM((2, 2 * width, width // 2), F32),
                pltpu.VMEM((2 * width, width // 2), F32),
                pltpu.VMEM((2 * width, width // 2), F32),
                pltpu.VMEM((2 * width, width // 2), F32),
                pltpu.VMEM((2, 2 * width, width // 2), F32),
                pltpu.SemaphoreType.DMA((10,)),
                pltpu.SemaphoreType.DMA((10,)),
                pltpu.SemaphoreType.DMA((8,)),
                pltpu.SemaphoreType.REGULAR,
            ],
            compiler_params=pltpu.CompilerParams(
                collective_id=0, has_side_effects=True, vmem_limit_bytes=48 << 20
            ),
        )(*given)
        return pl.pallas_call(
            write_out,
            out_shape=tuple(jax.ShapeDtypeStruct(x.shape, x.dtype) for x in results),
            in_specs=[whole] * 3,
            out_specs=(pl.BlockSpec(memory_space=pltpu.HBM),) * 3,
            scratch_shapes=[pltpu.SemaphoreType.DMA((3,))],
            compiler_params=pltpu.CompilerParams(vmem_limit_bytes=8 << 20),
        )(*[pltpu.with_memory_space_constraint(x, pltpu.VMEM) for x in results])

    placed = (
        P("dev", None),
        P("dev"),
        P(),
        P(),
        P("dev", None),
        P("dev", None, None),
        P("dev", None, None),
        P("dev", None),
    )
    return jax.shard_map(
        body, mesh=mesh, in_specs=placed, out_specs=(P("dev", None), P(), P()), check_vma=False
    )
```

```python
import functools

import jax
import jax.numpy as jnp
from jax import lax
from jax.experimental import pallas as pl
from jax.experimental.pallas import tpu as pltpu
from jax.sharding import PartitionSpec as P

MESH = pl.DeviceIdType.MESH
F32, BF16 = jnp.float32, jnp.bfloat16
PAIR_IN, SCATTER, GATHER, PAIR_OUT = range(4)
UNITS_A, UNITS_B, UNITS_C = ((0,), (1,)), ((0,), (1,)), ((0,), (1,))
UNITS = UNITS_A + UNITS_B + UNITS_C


SIDE = 4


def far_first():
    left = [(z, x, y) for z in range(SIDE) for x in range(SIDE) for y in range(SIDE)][1:]
    runs = []
    while left:
        z, x, y = left[0]
        run = []
        for step in ((z, x, y), (x, y, z), (y, z, x)):
            for there in (step, tuple(-v % SIDE for v in step)):
                if there not in run:
                    run.append(there)
        left = [there for there in left if there not in run]
        runs.append(run)
    return sorted(runs, key=lambda run: -sum(min(v, SIDE - v) for v in run[0]))


def split(x):
    high = x.astype(BF16)
    return high, (x - high.astype(F32)).astype(BF16)


def dot(left, right, dims=((1,), (0,))):
    return lax.dot_general(left, right, (dims, ((), ())), preferred_element_type=F32)


def pick(onehot, x):
    high, low = split(x)
    return dot(onehot, high) + dot(onehot, low)


def matmul(left, right, dims=((1,), (0,))):
    lh, ll = split(left)
    rh, rl = split(right)
    return dot(lh, rh, dims) + (dot(lh, rl, dims) + dot(ll, rh, dims))


def kernel(
    n, slots, *refs,
):
    given, (grad_features, grad_one, grad_two), held = refs[:8], refs[8:11], refs[11:19]
    (
        gather, spread, meet, terms, partner, pair_sum, parts, total, send_sem, recv_sem, load_sem, *boxes,
    ) = refs[19:]
    features, keep, theta_one, theta_two, cotangent, send_node, recv_edge, send_count = held
    loads = [pltpu.make_async_copy(given[i], held[i], load_sem.at[i]) for i in range(8)]
    for i in (5, 7, 6, 1, 0, 4, 2, 3):
        loads[i].start()
    me = lax.axis_index("dev")
    core, chip, chips = lax.rem(me, 2), me // 2, n // 2
    other = me + 1 - 2 * core
    place = (me // (2 * SIDE * SIDE), lax.rem(me // (2 * SIDE), SIDE), lax.rem(chip, SIDE))
    along = [
        [lax.rem(place[axis] + v, SIDE) * pitch for v in range(SIDE)]
        for axis, pitch in enumerate((2 * SIDE * SIDE, 2 * SIDE, 2))
    ]
    cores = (core, 1 - core)

    def peers(which):
        for run in far_first():
            for c in which:
                for z, x, y in run:
                    yield along[0][z] + along[1][x] + along[2][y] + c
    nodes, width = features.shape
    lanes = width // 2
    tile = 2 * slots

    barrier = pltpu.get_barrier_semaphore()
    for peer in [*peers(cores), other]:
        pl.semaphore_signal(barrier, inc=1, device_id=(peer,), device_id_type=MESH)

    def block(index, rows=tile):
        return pl.ds(pl.multiple_of(index * rows, rows), rows)

    def exchange(phase, src, dst):
        for peer in [*peers(cores), other]:
            pltpu.make_async_remote_copy(
                src_ref=src.at[peer],
                dst_ref=dst.at[me],
                send_sem=send_sem.at[phase],
                recv_sem=recv_sem.at[phase],
                device_id=(peer,),
                device_id_type=MESH,
            ).start()
        pltpu.make_async_copy(src.at[me], dst.at[me], recv_sem.at[phase]).start()

    def chip_exchange(phase, src_block, dst):
        for peer in peers((core,)):
            pltpu.make_async_remote_copy(
                src_ref=src_block(peer // 2),
                dst_ref=dst.at[block(chip)],
                send_sem=send_sem.at[phase],
                recv_sem=recv_sem.at[phase],
                device_id=(peer,),
                device_id_type=MESH,
            ).start()
        pltpu.make_async_copy(src_block(chip), dst.at[block(chip)], recv_sem.at[phase]).start()

    def arrived(phase, ref):
        pltpu.make_async_copy(ref, ref, recv_sem.at[phase]).wait()

    def sent(phase, ref):
        pltpu.make_async_copy(ref, ref, send_sem.at[phase]).wait()

    down, there, up, here_again = (boxes[k :: 4] for k in range(4))
    first_b, first_c = len(UNITS_A), len(UNITS_A) + len(UNITS_B)
    units_a, units_b, units_c = range(first_b), range(first_b, first_c), range(first_c, len(UNITS))

    def put(ref, j, rows):
        for h in range(rows.shape[1] // lanes):
            ref[:, h * slots + j, :] = rows[:, h * lanes : (h + 1) * lanes]

    def get(ref, j):
        return [ref[:, h * slots + j, :] for h in range(ref.shape[1] // slots)]

    def take(ref):
        return jnp.concatenate([jnp.concatenate(get(ref, j), axis=1) for j in range(slots)], axis=0)

    def columns(x, u):
        return x[:, UNITS[u][0] * lanes : (UNITS[u][-1] + 1) * lanes]

    eye = lax.broadcasted_iota(jnp.int32, (n, n), 0) == lax.broadcasted_iota(jnp.int32, (n, n), 1)

    def as_row(column):
        return jnp.sum(jnp.where(eye, column, 0.0), axis=0, keepdims=True)

    def as_column(row):
        return jnp.sum(jnp.where(eye, row, 0.0), axis=1, keepdims=True)

    for i in (5, 7, 6, 1):
        loads[i].wait()
    count = send_count[...].astype(F32)
    node_of = send_node[0].astype(F32)
    edge_of = recv_edge[0].astype(F32)
    node_lane = lax.broadcasted_iota(jnp.int32, (n, nodes), 1).astype(F32)
    node_row = lax.broadcasted_iota(jnp.int32, (nodes, n), 0).astype(F32)
    degree = jnp.zeros((nodes, n), F32)
    live = []
    for j in range(slots):
        mine = jnp.where(count > j, node_of[j : j + 1], -1.0)
        mine_column = as_column(mine)
        live.append(mine_column >= 0.0)
        gather[j * n : (j + 1) * n, :] = (node_lane == mine_column).astype(F32).astype(BF16)
        here = (node_row == mine).astype(F32)
        degree += here
        spread[:, j * n : (j + 1) * n] = here.astype(BF16)
    edge_cols = [as_column(edge_of[j : j + 1]) for j in range(slots)]
    edge_row = jnp.concatenate([edge_of[j : j + 1] for j in range(slots)], axis=1)
    for j in range(slots):
        meet[j * n : (j + 1) * n, :] = (edge_row == edge_cols[j]).astype(F32).astype(BF16)
    degree = jnp.sum(degree, axis=1, keepdims=True)
    node_scale = 1.0 / jnp.sqrt(jnp.maximum(degree, 1.0))
    keep_rows = keep[...].astype(F32)
    keep_f = jnp.concatenate([as_column(keep_rows[r : r + 1]) for r in range(nodes // n)], axis=0)

    def load_out(u, field):
        rows = pick(gather[...], columns(field, u) * node_scale)
        for j in range(slots):
            part = rows[j * n : (j + 1) * n]
            put(down[u], j, jnp.where(live[j], part, jnp.inf) if u == 0 else part)

    def send_down(u):
        exchange(2 * u + 4, down[u], there[u])

    def send_up(u):
        exchange(2 * u + 5, up[u], here_again[u])

    loads[0].wait()
    dropped = features[...] * keep_f
    for u in units_a:
        load_out(u, dropped)
    loads[4].wait()
    for u in units_b:
        load_out(u, cotangent[...])
    pl.semaphore_wait(barrier, n - 1)
    for u in (*units_a, *units_b):
        send_down(u)

    def load_up(u, field):
        rows = pick(meet[...], field)
        for j in range(slots):
            put(up[u], j, rows[j * n : (j + 1) * n] * edge_scale[j])

    edge_scale = []
    for u in (*units_a, *units_b):
        arrived(2 * u + 4, there[u])
        if u == 0:
            fields, alive = [], []
            for j in range(slots):
                pieces = get(there[u], j)
                is_live = pieces[0][:, :1] < jnp.inf
                alive.append(is_live.astype(F32))
                fields.append(jnp.where(is_live, jnp.concatenate(pieces, axis=1), 0.0))
            field = jnp.concatenate(fields, axis=0)
            alive_row = jnp.concatenate([as_row(a) for a in alive], axis=1)
            for j in range(slots):
                shared = jnp.where(edge_row == edge_cols[j], alive_row, 0.0)
                edge_scale.append(1.0 / jnp.maximum(jnp.sum(shared, axis=1, keepdims=True), 1.0))
        else:
            field = take(there[u])
        load_up(u, field)
        send_up(u)

    def propagated(u):
        arrived(2 * u + 5, here_again[u])
        return pick(spread[...], take(here_again[u])) * node_scale

    def set_term(k, halves, term):
        for i, h in enumerate(halves):
            terms[k, h * width : (h + 1) * width, :] = term[:, i * lanes : (i + 1) * lanes]

    spread_in = jnp.concatenate([propagated(u) for u in units_a], axis=1)
    loads[2].wait()
    loads[3].wait()
    pre = matmul(spread_in, theta_one[...])
    grow = jnp.exp(jnp.minimum(pre, 0.0))
    hidden = jnp.where(pre > 0, pre, grow - 1.0)
    slope = jnp.where(pre > 0, 1.0, grow)
    hidden_t, spread_in_t = hidden.T, spread_in.T
    pulled = 0.0
    for u in units_b:
        spread_cot = propagated(u)
        pulled += matmul(spread_cot, columns(theta_two[...], u), ((1,), (1,)))
        if u != units_b[-1]:
            set_term(1, UNITS[u], matmul(hidden_t, spread_cot))
    grad_pre = pulled * slope
    load_out(units_c[0], grad_pre)
    send_down(units_c[0])

    set_term(1, UNITS[units_b[-1]], matmul(hidden_t, spread_cot))
    set_term(0, (0, 1), matmul(spread_in_t, grad_pre))
    pltpu.make_async_remote_copy(
        src_ref=terms.at[1 - core],
        dst_ref=partner,
        send_sem=send_sem.at[PAIR_IN],
        recv_sem=recv_sem.at[PAIR_IN],
        device_id=(other,),
        device_id_type=MESH,
    ).start()
    for u in units_c[1:]:
        load_out(u, grad_pre)
        send_down(u)
    arrived(PAIR_IN, partner)
    pair_sum[...] = terms[core] + partner[...]
    chip_exchange(SCATTER, lambda q: pair_sum.at[block(q)], parts)

    for u in units_c:
        arrived(2 * u + 4, there[u])
        load_up(u, take(there[u]))
        send_up(u)

    arrived(SCATTER, parts)
    sent(SCATTER, parts.at[pl.ds(0, (chips - 1) * tile)])
    norm_factor = 1.0 / jnp.sqrt(jnp.float32(nodes * n))
    summed = jnp.sum(parts[...].reshape(chips, tile, lanes), axis=0) * norm_factor
    pair_sum[:tile, :] = summed
    chip_exchange(GATHER, lambda q: pair_sum.at[pl.ds(0, tile)], total.at[core])

    pulled = 0.0
    for u in units_c:
        pulled += matmul(propagated(u), columns(theta_one[...], u), ((1,), (1,)))
    grad_features[...] = pulled * keep_f

    arrived(GATHER, total.at[core])
    pltpu.make_async_remote_copy(
        src_ref=total.at[core],
        dst_ref=total.at[core],
        send_sem=send_sem.at[PAIR_OUT],
        recv_sem=recv_sem.at[PAIR_OUT],
        device_id=(other,),
        device_id_type=MESH,
    ).start()
    for u in range(len(UNITS)):
        sent(2 * u + 4, down[u].at[pl.ds(0, n - 1)])
        sent(2 * u + 5, up[u].at[pl.ds(0, n - 1)])
    sent(PAIR_IN, partner)
    sent(GATHER, parts.at[pl.ds(0, (chips - 1) * tile)])
    sent(PAIR_OUT, partner)
    arrived(PAIR_OUT, partner)
    for k, ref in enumerate((grad_one, grad_two)):
        for h in range(2):
            ref[:, h * lanes : (h + 1) * lanes] = total[k, h * width : (h + 1) * width, :]


def write_out(*refs):
    copies = [pltpu.make_async_copy(refs[i], refs[3 + i], refs[6].at[i]) for i in range(3)]
    for copy in copies:
        copy.start()
    for copy in copies:
        copy.wait()


def solution(mesh):
    n = mesh.shape["dev"]

    def body(features, keep, theta_one, theta_two, cotangent, send_node, recv_edge, send_count):
        nodes, width = features.shape
        slots = send_node.shape[2]
        whole = pl.BlockSpec(memory_space=pltpu.VMEM)
        given = (
            features, keep.reshape(nodes // n, n), theta_one, theta_two, cotangent,
            send_node.transpose(0, 2, 1), recv_edge.transpose(0, 2, 1), send_count,
        )
        given = [pltpu.with_memory_space_constraint(x, pltpu.HBM) for x in given]
        results = pl.pallas_call(
            functools.partial(kernel, n, slots),
            out_shape=(
                jax.ShapeDtypeStruct((nodes, width), F32),
                jax.ShapeDtypeStruct((width, width), F32),
                jax.ShapeDtypeStruct((width, width), F32),
            ),
            in_specs=[pl.BlockSpec(memory_space=pltpu.HBM)] * 8,
            out_specs=(whole,) * 3,
            scratch_shapes=[pltpu.VMEM(x.shape, x.dtype) for x in given]
            + [
                pltpu.VMEM((slots * n, nodes), BF16),
                pltpu.VMEM((nodes, slots * n), BF16),
                pltpu.VMEM((slots * n, slots * n), BF16),
                pltpu.VMEM((2, 2 * width, width // 2), F32),
                pltpu.VMEM((2 * width, width // 2), F32),
                pltpu.VMEM((2 * width, width // 2), F32),
                pltpu.VMEM((2 * width, width // 2), F32),
                pltpu.VMEM((2, 2 * width, width // 2), F32),
                pltpu.SemaphoreType.DMA((4 + 2 * len(UNITS),)),
                pltpu.SemaphoreType.DMA((4 + 2 * len(UNITS),)),
                pltpu.SemaphoreType.DMA((8,)),
            ]
            + [pltpu.VMEM((n, len(unit) * slots, width // 2), F32) for unit in UNITS for _ in range(4)],
            compiler_params=pltpu.CompilerParams(
                collective_id=0, has_side_effects=True, vmem_limit_bytes=48 << 20
            ),
        )(*given)
        return pl.pallas_call(
            write_out,
            out_shape=tuple(jax.ShapeDtypeStruct(x.shape, x.dtype) for x in results),
            in_specs=[whole] * 3,
            out_specs=(pl.BlockSpec(memory_space=pltpu.HBM),) * 3,
            scratch_shapes=[pltpu.SemaphoreType.DMA((3,))],
            compiler_params=pltpu.CompilerParams(vmem_limit_bytes=8 << 20),
        )(*[pltpu.with_memory_space_constraint(x, pltpu.VMEM) for x in results])

    placed = (
        P("dev", None),
        P("dev"),
        P(),
        P(),
        P("dev", None),
        P("dev", None, None),
        P("dev", None, None),
        P("dev", None),
    )
    return jax.shard_map(
        body, mesh=mesh, in_specs=placed, out_specs=(P("dev", None), P(), P()), check_vma=False
    )
```

```python
import functools

import jax
import jax.numpy as jnp
from jax import lax
from jax.experimental import pallas as pl
from jax.experimental.pallas import tpu as pltpu
from jax.sharding import PartitionSpec as P

MESH = pl.DeviceIdType.MESH
F32, BF16 = jnp.float32, jnp.bfloat16
PAIR_IN, SCATTER, GATHER, PAIR_OUT = range(4)
UNITS_A, UNITS_B, UNITS_C = ((0,), (1,)), ((0,), (1,)), ((0,), (1,))
UNITS = UNITS_A + UNITS_B + UNITS_C


SIDE = 4


def far_first():
    left = [(z, x, y) for z in range(SIDE) for x in range(SIDE) for y in range(SIDE)][1:]
    runs = []
    while left:
        z, x, y = left[0]
        run = []
        for step in ((z, x, y), (x, y, z), (y, z, x)):
            for there in (step, tuple(-v % SIDE for v in step)):
                if there not in run:
                    run.append(there)
        left = [there for there in left if there not in run]
        runs.append(run)
    return sorted(runs, key=lambda run: -sum(min(v, SIDE - v) for v in run[0]))


def split(x):
    high = x.astype(BF16)
    return high, (x - high.astype(F32)).astype(BF16)


def dot(left, right, dims=((1,), (0,))):
    return lax.dot_general(left, right, (dims, ((), ())), preferred_element_type=F32)


def pick(onehot, x):
    high, low = split(x)
    return dot(onehot, high) + dot(onehot, low)


def matmul(left, right, dims=((1,), (0,))):
    (lh, ll), (rh, rl) = left, right
    return dot(lh, rh, dims) + (dot(lh, rl, dims) + dot(ll, rh, dims))


def kernel(
    n, slots, *refs,
):
    given, (grad_features, grad_one, grad_two), held = refs[:8], refs[8:11], refs[11:19]
    (
        gather, spread, meet, terms, partner, pair_sum, parts, total, send_sem, recv_sem, load_sem, *boxes,
    ) = refs[19:]
    features, keep, theta_one, theta_two, cotangent, send_node, recv_edge, send_count = held
    loads = [pltpu.make_async_copy(given[i], held[i], load_sem.at[i]) for i in range(8)]
    for i in (5, 7, 1):
        loads[i].start()
    me = lax.axis_index("dev")
    core, chip, chips = lax.rem(me, 2), me // 2, n // 2
    other = me + 1 - 2 * core
    place = (me // (2 * SIDE * SIDE), lax.rem(me // (2 * SIDE), SIDE), lax.rem(chip, SIDE))
    along = [
        [lax.rem(place[axis] + v, SIDE) * pitch for v in range(SIDE)]
        for axis, pitch in enumerate((2 * SIDE * SIDE, 2 * SIDE, 2))
    ]
    cores = (core, 1 - core)

    def peers(which):
        for run in far_first():
            for c in which:
                for z, x, y in run:
                    yield along[0][z] + along[1][x] + along[2][y] + c
    nodes, width = features.shape
    lanes = width // 2
    tile = 2 * slots

    barrier = pltpu.get_barrier_semaphore()
    for peer in [*peers(cores), other]:
        pl.semaphore_signal(barrier, inc=1, device_id=(peer,), device_id_type=MESH)
    for i in (0, 4, 6, 2, 3):
        loads[i].start()

    def block(index, rows=tile):
        return pl.ds(pl.multiple_of(index * rows, rows), rows)

    def exchange(phase, src, dst):
        for peer in [*peers(cores), other]:
            pltpu.make_async_remote_copy(
                src_ref=src.at[peer],
                dst_ref=dst.at[me],
                send_sem=send_sem.at[phase],
                recv_sem=recv_sem.at[phase],
                device_id=(peer,),
                device_id_type=MESH,
            ).start()
        pltpu.make_async_copy(src.at[me], dst.at[me], recv_sem.at[phase]).start()

    def chip_exchange(phase, src_block, dst):
        for peer in peers((core,)):
            pltpu.make_async_remote_copy(
                src_ref=src_block(peer // 2),
                dst_ref=dst.at[block(chip)],
                send_sem=send_sem.at[phase],
                recv_sem=recv_sem.at[phase],
                device_id=(peer,),
                device_id_type=MESH,
            ).start()
        pltpu.make_async_copy(src_block(chip), dst.at[block(chip)], recv_sem.at[phase]).start()

    def arrived(phase, ref):
        pltpu.make_async_copy(ref, ref, recv_sem.at[phase]).wait()

    def sent(phase, ref):
        pltpu.make_async_copy(ref, ref, send_sem.at[phase]).wait()

    down, there, up, here_again = (boxes[k :: 4] for k in range(4))
    first_b, first_c = len(UNITS_A), len(UNITS_A) + len(UNITS_B)
    units_a, units_b, units_c = range(first_b), range(first_b, first_c), range(first_c, len(UNITS))

    def put(ref, j, rows):
        for h in range(rows.shape[1] // lanes):
            ref[:, h * slots + j, :] = rows[:, h * lanes : (h + 1) * lanes]

    def get(ref, j):
        return [ref[:, h * slots + j, :] for h in range(ref.shape[1] // slots)]

    def take(ref):
        return jnp.concatenate([jnp.concatenate(get(ref, j), axis=1) for j in range(slots)], axis=0)

    def columns(x, u):
        return x[:, UNITS[u][0] * lanes : (UNITS[u][-1] + 1) * lanes]

    eye = lax.broadcasted_iota(jnp.int32, (n, n), 0) == lax.broadcasted_iota(jnp.int32, (n, n), 1)

    def as_row(column):
        return jnp.sum(jnp.where(eye, column, 0.0), axis=0, keepdims=True)

    def as_column(row):
        return jnp.sum(jnp.where(eye, row, 0.0), axis=1, keepdims=True)

    for i in (5, 7, 1):
        loads[i].wait()
    count = send_count[...].astype(F32)
    node_of = send_node[0].astype(F32)
    node_lane = lax.broadcasted_iota(jnp.int32, (n, nodes), 1).astype(F32)
    node_row = lax.broadcasted_iota(jnp.int32, (nodes, n), 0).astype(F32)
    degree = jnp.zeros((nodes, n), F32)
    live = []
    for j in range(slots):
        mine = jnp.where(count > j, node_of[j : j + 1], -1.0)
        mine_column = as_column(mine)
        live.append(mine_column >= 0.0)
        gather[j * n : (j + 1) * n, :] = (node_lane == mine_column).astype(F32).astype(BF16)
        here = (node_row == mine).astype(F32)
        degree += here
        spread[:, j * n : (j + 1) * n] = here.astype(BF16)
    degree = jnp.sum(degree, axis=1, keepdims=True)
    node_scale = 1.0 / jnp.sqrt(jnp.maximum(degree, 1.0))
    keep_rows = keep[...].astype(F32)
    keep_f = jnp.concatenate([as_column(keep_rows[r : r + 1]) for r in range(nodes // n)], axis=0)

    def load_out(u, field):
        rows = pick(gather[...], columns(field, u) * node_scale)
        for j in range(slots):
            part = rows[j * n : (j + 1) * n]
            put(down[u], j, jnp.where(live[j], part, jnp.inf) if u == 0 else part)

    def send_down(u):
        exchange(2 * u + 4, down[u], there[u])

    def send_up(u):
        exchange(2 * u + 5, up[u], here_again[u])

    loads[0].wait()
    dropped = features[...] * keep_f
    for u in units_a:
        load_out(u, dropped)
    pl.semaphore_wait(barrier, n - 1)
    for u in units_a:
        send_down(u)
    loads[4].wait()
    for u in units_b:
        load_out(u, cotangent[...])
        send_down(u)

    loads[6].wait()
    edge_of = recv_edge[0].astype(F32)
    edge_cols = [as_column(edge_of[j : j + 1]) for j in range(slots)]
    edge_row = jnp.concatenate([edge_of[j : j + 1] for j in range(slots)], axis=1)
    for j in range(slots):
        meet[j * n : (j + 1) * n, :] = (edge_row == edge_cols[j]).astype(F32).astype(BF16)
    loads[2].wait()
    loads[3].wait()
    theta_one_split = split(theta_one[...])
    theta_two_split = split(theta_two[...])

    def load_up(u, field):
        rows = pick(meet[...], field)
        for j in range(slots):
            put(up[u], j, rows[j * n : (j + 1) * n] * edge_scale[j])

    edge_scale = []
    for u in (*units_a, *units_b):
        arrived(2 * u + 4, there[u])
        if u == 0:
            fields, alive = [], []
            for j in range(slots):
                pieces = get(there[u], j)
                is_live = pieces[0][:, :1] < jnp.inf
                alive.append(is_live.astype(F32))
                fields.append(jnp.where(is_live, jnp.concatenate(pieces, axis=1), 0.0))
            field = jnp.concatenate(fields, axis=0)
            alive_row = jnp.concatenate([as_row(a) for a in alive], axis=1)
            for j in range(slots):
                shared = jnp.where(edge_row == edge_cols[j], alive_row, 0.0)
                edge_scale.append(1.0 / jnp.maximum(jnp.sum(shared, axis=1, keepdims=True), 1.0))
        else:
            field = take(there[u])
        load_up(u, field)
        send_up(u)

    def propagated(u):
        arrived(2 * u + 5, here_again[u])
        return pick(spread[...], take(here_again[u])) * node_scale

    def set_term(k, halves, term):
        for i, h in enumerate(halves):
            terms[k, h * width : (h + 1) * width, :] = term[:, i * lanes : (i + 1) * lanes]

    spread_in = jnp.concatenate([propagated(u) for u in units_a], axis=1)
    pre = matmul(split(spread_in), theta_one_split)
    below = jnp.minimum(pre, 0.0)
    grow = jnp.exp(below)
    series = 1.0 + below / 7
    for k in (6, 5, 4, 3, 2):
        series = 1.0 + below * series * (1.0 / k)
    hidden = jnp.where(pre > 0, pre, jnp.where(below > -0.25, below * series, grow - 1.0))
    slope = jnp.where(pre > 0, 1.0, grow)
    hidden_t, spread_in_t = split(hidden.T), split(spread_in.T)
    pulled = 0.0
    for u in units_b:
        spread_cot = split(propagated(u))
        pulled += matmul(spread_cot, [columns(x, u) for x in theta_two_split], ((1,), (1,)))
        if u != units_b[-1]:
            set_term(1, UNITS[u], matmul(hidden_t, spread_cot))
    grad_pre = pulled * slope
    load_out(units_c[0], grad_pre)
    send_down(units_c[0])

    set_term(1, UNITS[units_b[-1]], matmul(hidden_t, spread_cot))
    set_term(0, (0, 1), matmul(spread_in_t, split(grad_pre)))
    pltpu.make_async_remote_copy(
        src_ref=terms.at[1 - core],
        dst_ref=partner,
        send_sem=send_sem.at[PAIR_IN],
        recv_sem=recv_sem.at[PAIR_IN],
        device_id=(other,),
        device_id_type=MESH,
    ).start()
    for u in units_c[1:]:
        load_out(u, grad_pre)
        send_down(u)
    arrived(PAIR_IN, partner)
    pair_sum[...] = terms[core] + partner[...]
    chip_exchange(SCATTER, lambda q: pair_sum.at[block(q)], parts)

    for u in units_c:
        arrived(2 * u + 4, there[u])
        load_up(u, take(there[u]))
        send_up(u)

    arrived(SCATTER, parts)
    sent(SCATTER, parts.at[pl.ds(0, (chips - 1) * tile)])
    norm_factor = 1.0 / jnp.sqrt(jnp.float32(nodes * n))
    summed = jnp.sum(parts[...].reshape(chips, tile, lanes), axis=0) * norm_factor
    pair_sum[:tile, :] = summed
    chip_exchange(GATHER, lambda q: pair_sum.at[pl.ds(0, tile)], total.at[core])

    pulled = 0.0
    for u in units_c:
        pulled += matmul(split(propagated(u)), [columns(x, u) for x in theta_one_split], ((1,), (1,)))
    grad_features[...] = pulled * keep_f

    arrived(GATHER, total.at[core])
    pltpu.make_async_remote_copy(
        src_ref=total.at[core],
        dst_ref=total.at[core],
        send_sem=send_sem.at[PAIR_OUT],
        recv_sem=recv_sem.at[PAIR_OUT],
        device_id=(other,),
        device_id_type=MESH,
    ).start()
    for u in range(len(UNITS)):
        sent(2 * u + 4, down[u].at[pl.ds(0, n - 1)])
        sent(2 * u + 5, up[u].at[pl.ds(0, n - 1)])
    sent(PAIR_IN, partner)
    sent(GATHER, parts.at[pl.ds(0, (chips - 1) * tile)])
    sent(PAIR_OUT, partner)
    arrived(PAIR_OUT, partner)
    for k, ref in enumerate((grad_one, grad_two)):
        for h in range(2):
            ref[:, h * lanes : (h + 1) * lanes] = total[k, h * width : (h + 1) * width, :]


def write_out(*refs):
    copies = [pltpu.make_async_copy(refs[i], refs[3 + i], refs[6].at[i]) for i in range(3)]
    for copy in copies:
        copy.start()
    for copy in copies:
        copy.wait()


def solution(mesh):
    n = mesh.shape["dev"]

    def body(features, keep, theta_one, theta_two, cotangent, send_node, recv_edge, send_count):
        nodes, width = features.shape
        slots = send_node.shape[2]
        whole = pl.BlockSpec(memory_space=pltpu.VMEM)
        given = (
            features, keep.reshape(nodes // n, n), theta_one, theta_two, cotangent,
            send_node.transpose(0, 2, 1), recv_edge.transpose(0, 2, 1), send_count,
        )
        given = [pltpu.with_memory_space_constraint(x, pltpu.HBM) for x in given]
        results = pl.pallas_call(
            functools.partial(kernel, n, slots),
            out_shape=(
                jax.ShapeDtypeStruct((nodes, width), F32),
                jax.ShapeDtypeStruct((width, width), F32),
                jax.ShapeDtypeStruct((width, width), F32),
            ),
            in_specs=[pl.BlockSpec(memory_space=pltpu.HBM)] * 8,
            out_specs=(whole,) * 3,
            scratch_shapes=[pltpu.VMEM(x.shape, x.dtype) for x in given]
            + [
                pltpu.VMEM((slots * n, nodes), BF16),
                pltpu.VMEM((nodes, slots * n), BF16),
                pltpu.VMEM((slots * n, slots * n), BF16),
                pltpu.VMEM((2, 2 * width, width // 2), F32),
                pltpu.VMEM((2 * width, width // 2), F32),
                pltpu.VMEM((2 * width, width // 2), F32),
                pltpu.VMEM((2 * width, width // 2), F32),
                pltpu.VMEM((2, 2 * width, width // 2), F32),
                pltpu.SemaphoreType.DMA((4 + 2 * len(UNITS),)),
                pltpu.SemaphoreType.DMA((4 + 2 * len(UNITS),)),
                pltpu.SemaphoreType.DMA((8,)),
            ]
            + [pltpu.VMEM((n, len(unit) * slots, width // 2), F32) for unit in UNITS for _ in range(4)],
            compiler_params=pltpu.CompilerParams(
                collective_id=0, has_side_effects=True, vmem_limit_bytes=48 << 20
            ),
        )(*given)
        return pl.pallas_call(
            write_out,
            out_shape=tuple(jax.ShapeDtypeStruct(x.shape, x.dtype) for x in results),
            in_specs=[whole] * 3,
            out_specs=(pl.BlockSpec(memory_space=pltpu.HBM),) * 3,
            scratch_shapes=[pltpu.SemaphoreType.DMA((3,))],
            compiler_params=pltpu.CompilerParams(vmem_limit_bytes=8 << 20),
        )(*[pltpu.with_memory_space_constraint(x, pltpu.VMEM) for x in results])

    placed = (
        P("dev", None),
        P("dev"),
        P(),
        P(),
        P("dev", None),
        P("dev", None, None),
        P("dev", None, None),
        P("dev", None),
    )
    return jax.shard_map(
        body, mesh=mesh, in_specs=placed, out_specs=(P("dev", None), P(), P()), check_vma=False
    )
```

```python
import functools

import jax
import jax.numpy as jnp
from jax import lax
from jax.experimental import pallas as pl
from jax.experimental.pallas import tpu as pltpu
from jax.sharding import PartitionSpec as P

MESH = pl.DeviceIdType.MESH
F32, BF16 = jnp.float32, jnp.bfloat16
PAIR_IN, SCATTER, GATHER, PAIR_OUT = range(4)
UNITS_A, UNITS_B, UNITS_C = ((0,), (1,)), ((0,), (1,)), ((0,), (1,))
UNITS = UNITS_A + UNITS_B + UNITS_C


SIDE = 4


def far_first():
    left = [(z, x, y) for z in range(SIDE) for x in range(SIDE) for y in range(SIDE)][1:]
    runs = []
    while left:
        z, x, y = left[0]
        run = []
        for step in ((z, x, y), (x, y, z), (y, z, x)):
            for there in (step, tuple(-v % SIDE for v in step)):
                if there not in run:
                    run.append(there)
        left = [there for there in left if there not in run]
        runs.append(run)
    return sorted(runs, key=lambda run: -sum(min(v, SIDE - v) for v in run[0]))


def split(x):
    high = x.astype(BF16)
    return high, (x - high.astype(F32)).astype(BF16)


def dot(left, right, dims=((1,), (0,))):
    return lax.dot_general(left, right, (dims, ((), ())), preferred_element_type=F32)


def pick(onehot, x):
    high, low = split(x)
    return dot(onehot, high) + dot(onehot, low)


def matmul(left, right, dims=((1,), (0,))):
    lh, ll = split(left)
    rh, rl = split(right)
    return dot(lh, rh, dims) + (dot(lh, rl, dims) + dot(ll, rh, dims))


def kernel(
    n, slots, *refs,
):
    given, (grad_features, grad_one, grad_two), held = refs[:8], refs[8:11], refs[11:19]
    (
        gather, spread, meet, terms, partner, pair_sum, parts, total, send_sem, recv_sem, load_sem, *boxes,
    ) = refs[19:]
    features, keep, theta_one, theta_two, cotangent, send_node, recv_edge, send_count = held
    loads = [pltpu.make_async_copy(given[i], held[i], load_sem.at[i]) for i in range(8)]
    for i in (5, 7, 6, 1, 0, 4, 2, 3):
        loads[i].start()
    me = lax.axis_index("dev")
    core, chip, chips = lax.rem(me, 2), me // 2, n // 2
    other = me + 1 - 2 * core
    place = (me // (2 * SIDE * SIDE), lax.rem(me // (2 * SIDE), SIDE), lax.rem(chip, SIDE))
    along = [
        [lax.rem(place[axis] + v, SIDE) * pitch for v in range(SIDE)]
        for axis, pitch in enumerate((2 * SIDE * SIDE, 2 * SIDE, 2))
    ]
    cores = (core, 1 - core)

    def peers(which):
        for run in far_first():
            for c in which:
                for z, x, y in run:
                    yield along[0][z] + along[1][x] + along[2][y] + c
    nodes, width = features.shape
    lanes = width // 2
    tile = 2 * slots

    barrier = pltpu.get_barrier_semaphore()
    for peer in [*peers(cores), other]:
        pl.semaphore_signal(barrier, inc=1, device_id=(peer,), device_id_type=MESH)

    def block(index, rows=tile):
        return pl.ds(pl.multiple_of(index * rows, rows), rows)

    def exchange(phase, src, dst):
        for peer in [*peers(cores), other]:
            pltpu.make_async_remote_copy(
                src_ref=src.at[peer],
                dst_ref=dst.at[me],
                send_sem=send_sem.at[phase],
                recv_sem=recv_sem.at[phase],
                device_id=(peer,),
                device_id_type=MESH,
            ).start()
        pltpu.make_async_copy(src.at[me], dst.at[me], recv_sem.at[phase]).start()

    def chip_exchange(phase, src_block, dst):
        for peer in peers((core,)):
            pltpu.make_async_remote_copy(
                src_ref=src_block(peer // 2),
                dst_ref=dst.at[block(chip)],
                send_sem=send_sem.at[phase],
                recv_sem=recv_sem.at[phase],
                device_id=(peer,),
                device_id_type=MESH,
            ).start()
        pltpu.make_async_copy(src_block(chip), dst.at[block(chip)], recv_sem.at[phase]).start()

    def arrived(phase, ref):
        pltpu.make_async_copy(ref, ref, recv_sem.at[phase]).wait()

    def sent(phase, ref):
        pltpu.make_async_copy(ref, ref, send_sem.at[phase]).wait()

    down, there, up, here_again = (boxes[k :: 4] for k in range(4))
    first_b, first_c = len(UNITS_A), len(UNITS_A) + len(UNITS_B)
    units_a, units_b, units_c = range(first_b), range(first_b, first_c), range(first_c, len(UNITS))

    def put(ref, j, rows):
        for h in range(rows.shape[1] // lanes):
            ref[:, h * slots + j, :] = rows[:, h * lanes : (h + 1) * lanes]

    def get(ref, j):
        return [ref[:, h * slots + j, :] for h in range(ref.shape[1] // slots)]

    def take(ref):
        return jnp.concatenate([jnp.concatenate(get(ref, j), axis=1) for j in range(slots)], axis=0)

    def columns(x, u):
        return x[:, UNITS[u][0] * lanes : (UNITS[u][-1] + 1) * lanes]

    eye = lax.broadcasted_iota(jnp.int32, (n, n), 0) == lax.broadcasted_iota(jnp.int32, (n, n), 1)

    def as_row(column):
        return jnp.sum(jnp.where(eye, column, 0.0), axis=0, keepdims=True)

    def as_column(row):
        return jnp.sum(jnp.where(eye, row, 0.0), axis=1, keepdims=True)

    for i in (5, 7, 6, 1):
        loads[i].wait()
    count = send_count[...].astype(F32)
    node_of = send_node[0].astype(F32)
    edge_of = recv_edge[0].astype(F32)
    node_lane = lax.broadcasted_iota(jnp.int32, (n, nodes), 1).astype(F32)
    node_row = lax.broadcasted_iota(jnp.int32, (nodes, n), 0).astype(F32)
    degree = jnp.zeros((nodes, n), F32)
    live = []
    for j in range(slots):
        mine = jnp.where(count > j, node_of[j : j + 1], -1.0)
        mine_column = as_column(mine)
        live.append(mine_column >= 0.0)
        gather[j * n : (j + 1) * n, :] = (node_lane == mine_column).astype(F32).astype(BF16)
        here = (node_row == mine).astype(F32)
        degree += here
        spread[:, j * n : (j + 1) * n] = here.astype(BF16)
    edge_cols = [as_column(edge_of[j : j + 1]) for j in range(slots)]
    edge_row = jnp.concatenate([edge_of[j : j + 1] for j in range(slots)], axis=1)
    for j in range(slots):
        meet[j * n : (j + 1) * n, :] = (edge_row == edge_cols[j]).astype(F32).astype(BF16)
    degree = jnp.sum(degree, axis=1, keepdims=True)
    node_scale = 1.0 / jnp.sqrt(jnp.maximum(degree, 1.0))
    keep_rows = keep[...].astype(F32)
    keep_f = jnp.concatenate([as_column(keep_rows[r : r + 1]) for r in range(nodes // n)], axis=0)

    def load_out(u, field):
        rows = pick(gather[...], columns(field, u) * node_scale)
        for j in range(slots):
            part = rows[j * n : (j + 1) * n]
            put(down[u], j, jnp.where(live[j], part, jnp.inf) if u == 0 else part)

    def send_down(u):
        exchange(2 * u + 4, down[u], there[u])

    def send_up(u):
        exchange(2 * u + 5, up[u], here_again[u])

    loads[0].wait()
    dropped = features[...] * keep_f
    for u in units_a:
        load_out(u, dropped)
    loads[4].wait()
    for u in units_b:
        load_out(u, cotangent[...])
    pl.semaphore_wait(barrier, n - 1)
    for u in (*units_a, *units_b):
        send_down(u)

    def load_up(u, field):
        rows = pick(meet[...], field)
        for j in range(slots):
            put(up[u], j, rows[j * n : (j + 1) * n] * edge_scale[j])

    edge_scale = []
    for u in (*units_a, *units_b):
        arrived(2 * u + 4, there[u])
        if u == 0:
            fields, alive = [], []
            for j in range(slots):
                pieces = get(there[u], j)
                is_live = pieces[0][:, :1] < jnp.inf
                alive.append(is_live.astype(F32))
                fields.append(jnp.where(is_live, jnp.concatenate(pieces, axis=1), 0.0))
            field = jnp.concatenate(fields, axis=0)
            alive_row = jnp.concatenate([as_row(a) for a in alive], axis=1)
            for j in range(slots):
                shared = jnp.where(edge_row == edge_cols[j], alive_row, 0.0)
                edge_scale.append(1.0 / jnp.maximum(jnp.sum(shared, axis=1, keepdims=True), 1.0))
        else:
            field = take(there[u])
        load_up(u, field)
        send_up(u)

    def propagated(u):
        arrived(2 * u + 5, here_again[u])
        return pick(spread[...], take(here_again[u])) * node_scale

    def set_term(k, halves, term):
        for i, h in enumerate(halves):
            terms[k, h * width : (h + 1) * width, :] = term[:, i * lanes : (i + 1) * lanes]

    spread_in = jnp.concatenate([propagated(u) for u in units_a], axis=1)
    loads[2].wait()
    loads[3].wait()
    pre = matmul(spread_in, theta_one[...])
    below = jnp.minimum(pre, 0.0)
    grow = jnp.exp(below)
    series = 1.0 + below / 7
    for k in (6, 5, 4, 3, 2):
        series = 1.0 + below * series * (1.0 / k)
    hidden = jnp.where(pre > 0, pre, jnp.where(below > -0.25, below * series, grow - 1.0))
    slope = jnp.where(pre > 0, 1.0, grow)
    hidden_t, spread_in_t = hidden.T, spread_in.T
    pulled = 0.0
    for u in units_b:
        spread_cot = propagated(u)
        pulled += matmul(spread_cot, columns(theta_two[...], u), ((1,), (1,)))
        if u != units_b[-1]:
            set_term(1, UNITS[u], matmul(hidden_t, spread_cot))
    grad_pre = pulled * slope
    load_out(units_c[0], grad_pre)
    send_down(units_c[0])

    set_term(1, UNITS[units_b[-1]], matmul(hidden_t, spread_cot))
    set_term(0, (0, 1), matmul(spread_in_t, grad_pre))
    pltpu.make_async_remote_copy(
        src_ref=terms.at[1 - core],
        dst_ref=partner,
        send_sem=send_sem.at[PAIR_IN],
        recv_sem=recv_sem.at[PAIR_IN],
        device_id=(other,),
        device_id_type=MESH,
    ).start()
    for u in units_c[1:]:
        load_out(u, grad_pre)
        send_down(u)
    arrived(PAIR_IN, partner)
    pair_sum[...] = terms[core] + partner[...]
    chip_exchange(SCATTER, lambda q: pair_sum.at[block(q)], parts)

    for u in units_c:
        arrived(2 * u + 4, there[u])
        load_up(u, take(there[u]))
        send_up(u)

    arrived(SCATTER, parts)
    sent(SCATTER, parts.at[pl.ds(0, (chips - 1) * tile)])
    norm_factor = 1.0 / jnp.sqrt(jnp.float32(nodes * n))
    summed = jnp.sum(parts[...].reshape(chips, tile, lanes), axis=0) * norm_factor
    pair_sum[:tile, :] = summed
    chip_exchange(GATHER, lambda q: pair_sum.at[pl.ds(0, tile)], total.at[core])

    pulled = 0.0
    for u in units_c:
        pulled += matmul(propagated(u), columns(theta_one[...], u), ((1,), (1,)))
    grad_features[...] = pulled * keep_f

    arrived(GATHER, total.at[core])
    pltpu.make_async_remote_copy(
        src_ref=total.at[core],
        dst_ref=total.at[core],
        send_sem=send_sem.at[PAIR_OUT],
        recv_sem=recv_sem.at[PAIR_OUT],
        device_id=(other,),
        device_id_type=MESH,
    ).start()
    for u in range(len(UNITS)):
        sent(2 * u + 4, down[u].at[pl.ds(0, n - 1)])
        sent(2 * u + 5, up[u].at[pl.ds(0, n - 1)])
    sent(PAIR_IN, partner)
    sent(GATHER, parts.at[pl.ds(0, (chips - 1) * tile)])
    sent(PAIR_OUT, partner)
    arrived(PAIR_OUT, partner)
    for k, ref in enumerate((grad_one, grad_two)):
        for h in range(2):
            ref[:, h * lanes : (h + 1) * lanes] = total[k, h * width : (h + 1) * width, :]


def write_out(*refs):
    copies = [pltpu.make_async_copy(refs[i], refs[3 + i], refs[6].at[i]) for i in range(3)]
    for copy in copies:
        copy.start()
    for copy in copies:
        copy.wait()


def solution(mesh):
    n = mesh.shape["dev"]

    def body(features, keep, theta_one, theta_two, cotangent, send_node, recv_edge, send_count):
        nodes, width = features.shape
        slots = send_node.shape[2]
        whole = pl.BlockSpec(memory_space=pltpu.VMEM)
        given = (
            features, keep.reshape(nodes // n, n), theta_one, theta_two, cotangent,
            send_node.transpose(0, 2, 1), recv_edge.transpose(0, 2, 1), send_count,
        )
        given = [pltpu.with_memory_space_constraint(x, pltpu.HBM) for x in given]
        results = pl.pallas_call(
            functools.partial(kernel, n, slots),
            out_shape=(
                jax.ShapeDtypeStruct((nodes, width), F32),
                jax.ShapeDtypeStruct((width, width), F32),
                jax.ShapeDtypeStruct((width, width), F32),
            ),
            in_specs=[pl.BlockSpec(memory_space=pltpu.HBM)] * 8,
            out_specs=(whole,) * 3,
            scratch_shapes=[pltpu.VMEM(x.shape, x.dtype) for x in given]
            + [
                pltpu.VMEM((slots * n, nodes), BF16),
                pltpu.VMEM((nodes, slots * n), BF16),
                pltpu.VMEM((slots * n, slots * n), BF16),
                pltpu.VMEM((2, 2 * width, width // 2), F32),
                pltpu.VMEM((2 * width, width // 2), F32),
                pltpu.VMEM((2 * width, width // 2), F32),
                pltpu.VMEM((2 * width, width // 2), F32),
                pltpu.VMEM((2, 2 * width, width // 2), F32),
                pltpu.SemaphoreType.DMA((4 + 2 * len(UNITS),)),
                pltpu.SemaphoreType.DMA((4 + 2 * len(UNITS),)),
                pltpu.SemaphoreType.DMA((8,)),
            ]
            + [pltpu.VMEM((n, len(unit) * slots, width // 2), F32) for unit in UNITS for _ in range(4)],
            compiler_params=pltpu.CompilerParams(
                collective_id=0, has_side_effects=True, vmem_limit_bytes=48 << 20
            ),
        )(*given)
        return pl.pallas_call(
            write_out,
            out_shape=tuple(jax.ShapeDtypeStruct(x.shape, x.dtype) for x in results),
            in_specs=[whole] * 3,
            out_specs=(pl.BlockSpec(memory_space=pltpu.HBM),) * 3,
            scratch_shapes=[pltpu.SemaphoreType.DMA((3,))],
            compiler_params=pltpu.CompilerParams(vmem_limit_bytes=8 << 20),
        )(*[pltpu.with_memory_space_constraint(x, pltpu.VMEM) for x in results])

    placed = (
        P("dev", None),
        P("dev"),
        P(),
        P(),
        P("dev", None),
        P("dev", None, None),
        P("dev", None, None),
        P("dev", None),
    )
    return jax.shard_map(
        body, mesh=mesh, in_specs=placed, out_specs=(P("dev", None), P(), P()), check_vma=False
    )
```

```python
import functools

import jax
import jax.numpy as jnp
from jax import lax
from jax.experimental import pallas as pl
from jax.experimental.pallas import tpu as pltpu
from jax.sharding import PartitionSpec as P

MESH = pl.DeviceIdType.MESH
F32, BF16 = jnp.float32, jnp.bfloat16
PAIR_IN, SCATTER, GATHER, PAIR_OUT = range(4)
UNITS_A, UNITS_B, UNITS_C = ((0,), (1,)), ((0,), (1,)), ((0,), (1,))
UNITS = UNITS_A + UNITS_B + UNITS_C


SIDE = 4


def far_first():
    left = [(z, x, y) for z in range(SIDE) for x in range(SIDE) for y in range(SIDE)][1:]
    runs = []
    while left:
        z, x, y = left[0]
        run = []
        for step in ((z, x, y), (x, y, z), (y, z, x)):
            for there in (step, tuple(-v % SIDE for v in step)):
                if there not in run:
                    run.append(there)
        left = [there for there in left if there not in run]
        runs.append(run)
    return sorted(runs, key=lambda run: -sum(min(v, SIDE - v) for v in run[0]))


def split(x):
    high = x.astype(BF16)
    return high, (x - high.astype(F32)).astype(BF16)


def dot(left, right, dims=((1,), (0,))):
    return lax.dot_general(left, right, (dims, ((), ())), preferred_element_type=F32)


def pick(onehot, x):
    high, low = split(x)
    return dot(onehot, high) + dot(onehot, low)


def matmul(left, right, dims=((1,), (0,))):
    lh, ll = split(left)
    rh, rl = split(right)
    return dot(lh, rh, dims) + (dot(lh, rl, dims) + dot(ll, rh, dims))


def kernel(
    n, slots, *refs,
):
    given, (grad_features, grad_one, grad_two), held = refs[:8], refs[8:11], refs[11:19]
    (
        gather, spread, meet, terms, partner, pair_sum, parts, total, send_sem, recv_sem, load_sem, *boxes,
    ) = refs[19:]
    features, keep, theta_one, theta_two, cotangent, send_node, recv_edge, send_count = held
    loads = [pltpu.make_async_copy(given[i], held[i], load_sem.at[i]) for i in range(8)]
    for i in (5, 7, 6, 1, 0, 4, 2, 3):
        loads[i].start()
    me = lax.axis_index("dev")
    core, chip, chips = lax.rem(me, 2), me // 2, n // 2
    other = me + 1 - 2 * core
    place = (me // (2 * SIDE * SIDE), lax.rem(me // (2 * SIDE), SIDE), lax.rem(chip, SIDE))
    along = [
        [lax.rem(place[axis] + v, SIDE) * pitch for v in range(SIDE)]
        for axis, pitch in enumerate((2 * SIDE * SIDE, 2 * SIDE, 2))
    ]
    cores = (core, 1 - core)

    def peers(which):
        for run in far_first():
            for c in which:
                for z, x, y in run:
                    yield along[0][z] + along[1][x] + along[2][y] + c
    nodes, width = features.shape
    lanes = width // 2
    tile = 2 * slots

    barrier = pltpu.get_barrier_semaphore()
    for peer in [*peers(cores), other]:
        pl.semaphore_signal(barrier, inc=1, device_id=(peer,), device_id_type=MESH)

    def block(index, rows=tile):
        return pl.ds(pl.multiple_of(index * rows, rows), rows)

    def exchange(phase, src, dst):
        for peer in [*peers(cores), other]:
            pltpu.make_async_remote_copy(
                src_ref=src.at[peer],
                dst_ref=dst.at[me],
                send_sem=send_sem.at[phase],
                recv_sem=recv_sem.at[phase],
                device_id=(peer,),
                device_id_type=MESH,
            ).start()
        pltpu.make_async_copy(src.at[me], dst.at[me], recv_sem.at[phase]).start()

    def chip_exchange(phase, src_block, dst):
        for peer in peers((core,)):
            pltpu.make_async_remote_copy(
                src_ref=src_block(peer // 2),
                dst_ref=dst.at[block(chip)],
                send_sem=send_sem.at[phase],
                recv_sem=recv_sem.at[phase],
                device_id=(peer,),
                device_id_type=MESH,
            ).start()
        pltpu.make_async_copy(src_block(chip), dst.at[block(chip)], recv_sem.at[phase]).start()

    def arrived(phase, ref):
        pltpu.make_async_copy(ref, ref, recv_sem.at[phase]).wait()

    def sent(phase, ref):
        pltpu.make_async_copy(ref, ref, send_sem.at[phase]).wait()

    down, there, up, here_again = (boxes[k :: 4] for k in range(4))
    first_b, first_c = len(UNITS_A), len(UNITS_A) + len(UNITS_B)
    units_a, units_b, units_c = range(first_b), range(first_b, first_c), range(first_c, len(UNITS))

    def put(ref, j, rows):
        for h in range(rows.shape[1] // lanes):
            ref[:, h * slots + j, :] = rows[:, h * lanes : (h + 1) * lanes]

    def get(ref, j):
        return [ref[:, h * slots + j, :] for h in range(ref.shape[1] // slots)]

    def take(ref):
        return jnp.concatenate([jnp.concatenate(get(ref, j), axis=1) for j in range(slots)], axis=0)

    def columns(x, u):
        return x[:, UNITS[u][0] * lanes : (UNITS[u][-1] + 1) * lanes]

    eye = lax.broadcasted_iota(jnp.int32, (n, n), 0) == lax.broadcasted_iota(jnp.int32, (n, n), 1)

    def as_row(column):
        return jnp.sum(jnp.where(eye, column, 0.0), axis=0, keepdims=True)

    def as_column(row):
        return jnp.sum(jnp.where(eye, row, 0.0), axis=1, keepdims=True)

    for i in (5, 7, 6, 1):
        loads[i].wait()
    count = send_count[...].astype(F32)
    node_of = send_node[0].astype(F32)
    edge_of = recv_edge[0].astype(F32)
    node_lane = lax.broadcasted_iota(jnp.int32, (n, nodes), 1).astype(F32)
    node_row = lax.broadcasted_iota(jnp.int32, (nodes, n), 0).astype(F32)
    degree = jnp.zeros((nodes, n), F32)
    live = []
    for j in range(slots):
        mine = jnp.where(count > j, node_of[j : j + 1], -1.0)
        mine_column = as_column(mine)
        live.append(mine_column >= 0.0)
        gather[j * n : (j + 1) * n, :] = (node_lane == mine_column).astype(F32).astype(BF16)
        here = (node_row == mine).astype(F32)
        degree += here
        spread[:, j * n : (j + 1) * n] = here.astype(BF16)
    edge_cols = [as_column(edge_of[j : j + 1]) for j in range(slots)]
    edge_row = jnp.concatenate([edge_of[j : j + 1] for j in range(slots)], axis=1)
    for j in range(slots):
        meet[j * n : (j + 1) * n, :] = (edge_row == edge_cols[j]).astype(F32).astype(BF16)
    degree = jnp.sum(degree, axis=1, keepdims=True)
    node_scale = 1.0 / jnp.sqrt(jnp.maximum(degree, 1.0))
    keep_rows = keep[...].astype(F32)
    keep_f = jnp.concatenate([as_column(keep_rows[r : r + 1]) for r in range(nodes // n)], axis=0)

    def channels(ref, u):
        return ref[UNITS[u][0] * lanes : (UNITS[u][-1] + 1) * lanes, :]

    def load_part(u, part):
        rows = pick(gather[...], part * node_scale)
        for j in range(slots):
            part = rows[j * n : (j + 1) * n]
            put(down[u], j, jnp.where(live[j], part, jnp.inf) if u == 0 else part)

    def load_out(u, field):
        load_part(u, columns(field, u))

    def send_down(u):
        exchange(2 * u + 4, down[u], there[u])

    def send_up(u):
        exchange(2 * u + 5, up[u], here_again[u])

    loads[0].wait()
    dropped = features[...] * keep_f
    for u in units_a:
        load_out(u, dropped)
    loads[4].wait()
    for u in units_b:
        load_out(u, cotangent[...])
    pl.semaphore_wait(barrier, n - 1)
    for u in (*units_a, *units_b):
        send_down(u)

    def load_up(u, field):
        rows = pick(meet[...], field)
        for j in range(slots):
            put(up[u], j, rows[j * n : (j + 1) * n] * edge_scale[j])

    edge_scale = []
    for u in (*units_a, *units_b):
        arrived(2 * u + 4, there[u])
        if u == 0:
            fields, alive = [], []
            for j in range(slots):
                pieces = get(there[u], j)
                is_live = pieces[0][:, :1] < jnp.inf
                alive.append(is_live.astype(F32))
                fields.append(jnp.where(is_live, jnp.concatenate(pieces, axis=1), 0.0))
            field = jnp.concatenate(fields, axis=0)
            alive_row = jnp.concatenate([as_row(a) for a in alive], axis=1)
            for j in range(slots):
                shared = jnp.where(edge_row == edge_cols[j], alive_row, 0.0)
                edge_scale.append(1.0 / jnp.maximum(jnp.sum(shared, axis=1, keepdims=True), 1.0))
        else:
            field = take(there[u])
        load_up(u, field)
        send_up(u)

    def propagated(u):
        arrived(2 * u + 5, here_again[u])
        return pick(spread[...], take(here_again[u])) * node_scale

    def set_term(k, halves, term):
        for i, h in enumerate(halves):
            terms[k, h * width : (h + 1) * width, :] = term[:, i * lanes : (i + 1) * lanes]

    spread_in = jnp.concatenate([propagated(u) for u in units_a], axis=1)
    loads[2].wait()
    loads[3].wait()
    pre = matmul(spread_in, theta_one[...])
    below = jnp.minimum(pre, 0.0)
    grow = jnp.exp(below)
    series = 1.0 + below / 7
    for k in (6, 5, 4, 3, 2):
        series = 1.0 + below * series * (1.0 / k)
    hidden = jnp.where(pre > 0, pre, jnp.where(below > -0.25, below * series, grow - 1.0))
    slope = jnp.where(pre > 0, 1.0, grow)
    hidden_t, spread_in_t = hidden.T, spread_in.T
    pulled = [0.0] * len(units_c)
    for u in units_b:
        spread_cot = propagated(u)
        if u != units_b[-1]:
            for k, c in enumerate(units_c):
                pulled[k] += matmul(spread_cot, columns(channels(theta_two, c), u), ((1,), (1,)))
            set_term(1, UNITS[u], matmul(hidden_t, spread_cot))

    def grad_part(c):
        pull = matmul(spread_cot, columns(channels(theta_two, c), units_b[-1]), ((1,), (1,)))
        return (pulled[c - first_c] + pull) * columns(slope, c)

    grad_parts = [grad_part(units_c[0])]
    load_part(units_c[0], grad_parts[0])
    send_down(units_c[0])
    grad_parts += [grad_part(c) for c in units_c[1:]]
    grad_pre = jnp.concatenate(grad_parts, axis=1)

    set_term(1, UNITS[units_b[-1]], matmul(hidden_t, spread_cot))
    set_term(0, (0, 1), matmul(spread_in_t, grad_pre))
    pltpu.make_async_remote_copy(
        src_ref=terms.at[1 - core],
        dst_ref=partner,
        send_sem=send_sem.at[PAIR_IN],
        recv_sem=recv_sem.at[PAIR_IN],
        device_id=(other,),
        device_id_type=MESH,
    ).start()
    for u in units_c[1:]:
        load_out(u, grad_pre)
        send_down(u)
    arrived(PAIR_IN, partner)
    pair_sum[...] = terms[core] + partner[...]
    chip_exchange(SCATTER, lambda q: pair_sum.at[block(q)], parts)

    for u in units_c:
        arrived(2 * u + 4, there[u])
        load_up(u, take(there[u]))
        send_up(u)

    arrived(SCATTER, parts)
    sent(SCATTER, parts.at[pl.ds(0, (chips - 1) * tile)])
    norm_factor = 1.0 / jnp.sqrt(jnp.float32(nodes * n))
    summed = jnp.sum(parts[...].reshape(chips, tile, lanes), axis=0) * norm_factor
    pair_sum[:tile, :] = summed
    chip_exchange(GATHER, lambda q: pair_sum.at[pl.ds(0, tile)], total.at[core])

    pulled = 0.0
    for u in units_c:
        pulled += matmul(propagated(u), columns(theta_one[...], u), ((1,), (1,)))
    grad_features[...] = pulled * keep_f

    arrived(GATHER, total.at[core])
    pltpu.make_async_remote_copy(
        src_ref=total.at[core],
        dst_ref=total.at[core],
        send_sem=send_sem.at[PAIR_OUT],
        recv_sem=recv_sem.at[PAIR_OUT],
        device_id=(other,),
        device_id_type=MESH,
    ).start()
    for u in range(len(UNITS)):
        sent(2 * u + 4, down[u].at[pl.ds(0, n - 1)])
        sent(2 * u + 5, up[u].at[pl.ds(0, n - 1)])
    sent(PAIR_IN, partner)
    sent(GATHER, parts.at[pl.ds(0, (chips - 1) * tile)])
    sent(PAIR_OUT, partner)
    arrived(PAIR_OUT, partner)
    for k, ref in enumerate((grad_one, grad_two)):
        for h in range(2):
            ref[:, h * lanes : (h + 1) * lanes] = total[k, h * width : (h + 1) * width, :]


def write_out(*refs):
    copies = [pltpu.make_async_copy(refs[i], refs[3 + i], refs[6].at[i]) for i in range(3)]
    for copy in copies:
        copy.start()
    for copy in copies:
        copy.wait()


def solution(mesh):
    n = mesh.shape["dev"]

    def body(features, keep, theta_one, theta_two, cotangent, send_node, recv_edge, send_count):
        nodes, width = features.shape
        slots = send_node.shape[2]
        whole = pl.BlockSpec(memory_space=pltpu.VMEM)
        given = (
            features, keep.reshape(nodes // n, n), theta_one, theta_two, cotangent,
            send_node.transpose(0, 2, 1), recv_edge.transpose(0, 2, 1), send_count,
        )
        given = [pltpu.with_memory_space_constraint(x, pltpu.HBM) for x in given]
        results = pl.pallas_call(
            functools.partial(kernel, n, slots),
            out_shape=(
                jax.ShapeDtypeStruct((nodes, width), F32),
                jax.ShapeDtypeStruct((width, width), F32),
                jax.ShapeDtypeStruct((width, width), F32),
            ),
            in_specs=[pl.BlockSpec(memory_space=pltpu.HBM)] * 8,
            out_specs=(whole,) * 3,
            scratch_shapes=[pltpu.VMEM(x.shape, x.dtype) for x in given]
            + [
                pltpu.VMEM((slots * n, nodes), BF16),
                pltpu.VMEM((nodes, slots * n), BF16),
                pltpu.VMEM((slots * n, slots * n), BF16),
                pltpu.VMEM((2, 2 * width, width // 2), F32),
                pltpu.VMEM((2 * width, width // 2), F32),
                pltpu.VMEM((2 * width, width // 2), F32),
                pltpu.VMEM((2 * width, width // 2), F32),
                pltpu.VMEM((2, 2 * width, width // 2), F32),
                pltpu.SemaphoreType.DMA((4 + 2 * len(UNITS),)),
                pltpu.SemaphoreType.DMA((4 + 2 * len(UNITS),)),
                pltpu.SemaphoreType.DMA((8,)),
            ]
            + [pltpu.VMEM((n, len(unit) * slots, width // 2), F32) for unit in UNITS for _ in range(4)],
            compiler_params=pltpu.CompilerParams(
                collective_id=0, has_side_effects=True, vmem_limit_bytes=48 << 20
            ),
        )(*given)
        return pl.pallas_call(
            write_out,
            out_shape=tuple(jax.ShapeDtypeStruct(x.shape, x.dtype) for x in results),
            in_specs=[whole] * 3,
            out_specs=(pl.BlockSpec(memory_space=pltpu.HBM),) * 3,
            scratch_shapes=[pltpu.SemaphoreType.DMA((3,))],
            compiler_params=pltpu.CompilerParams(vmem_limit_bytes=8 << 20),
        )(*[pltpu.with_memory_space_constraint(x, pltpu.VMEM) for x in results])

    placed = (
        P("dev", None),
        P("dev"),
        P(),
        P(),
        P("dev", None),
        P("dev", None, None),
        P("dev", None, None),
        P("dev", None),
    )
    return jax.shard_map(
        body, mesh=mesh, in_specs=placed, out_specs=(P("dev", None), P(), P()), check_vma=False
    )
```
